32 devices in a mesh: beam: 2 (over x), freq: 16 (over z, y, core).
Axes of the slice: x: 2, y: 2, z: 4, core: 2. Of those that a mesh axis runs over, the one named last changes fastest.
Arguments:
- spectra: float32 [512, 8192], P(('beam', 'freq')), parts along dimension 0, may hold values from -36 to 36
- profiles: bfloat16 [64, 256], replicated, may hold values from -0.375 to 0.375
- shifts: int32 [15, 32], replicated, may hold values from 0 to 512
Outputs:
- peaks: bfloat16 [512, 64, 64], P(('beam', 'freq')), parts along dimension 0
The draws below stay inside these ranges and needn't reach their ends.
There are 2 independent parts, one for each index of `beam`. The reference program is written for one: setup_inputs(seed, part) draws one part's arguments, and reference() takes and returns one part's arrays. A program takes and returns all parts, laid end to end along the dimension named above; an argument that names none is the same for every part. Nothing has to cross between parts.
All inputs are finite; a program needn't handle non-finite values.
Results may differ from the reference program's by a relative error of at most 0.0048.
Values sent between devices are 32-bit elements; how exact they have to be, the bound alone decides.
A program may use at most 64 MiB of HBM per device.

```python
import jax
import jax.numpy as jnp
from jax import lax

R = 16
TIME = 8192
PROFS = 64
TAPS = 256
STRIDE = 8
HOLD = 16
SUBBANDS = 16
MAXSHIFT = 512
PEAKS = 64


def draw_spectra(key, part):
    key_base = jax.random.fold_in(key, 11)
    key_gain = jax.random.fold_in(key, 23)
    row_total = SUBBANDS * R
    band_pos = jnp.arange(SUBBANDS, dtype=jnp.float32) / max(SUBBANDS - 1, 1)
    band_scale = 3.0 ** band_pos * jax.random.uniform(key_gain, (SUBBANDS,), jnp.float32, 1.0, 2.0)
    base_draw = jnp.clip(jax.random.normal(key_base, (row_total, TIME), jnp.float32), -6.0, 6.0)
    return (jnp.repeat(band_scale, R)[:, None] * base_draw).astype(jnp.float32)


def set_ends(entries, stream_key, least, largest):
    dims = entries.shape
    place = [jax.random.randint(jax.random.fold_in(stream_key, axis), (), 0, dims[axis]) for axis in range(len(dims))]
    entries = entries.at[tuple(place)].set(least)
    longest = dims.index(max(dims))
    place[longest] = (place[longest] + 1) % dims[longest]
    return entries.at[tuple(place)].set(largest)


def scatter_about(rng, extent, deviation, limit, held_as=jnp.bfloat16):
    array = deviation * jax.random.normal(rng, extent, jnp.float32)
    return jnp.clip(array, min=-limit, max=limit).astype(held_as)


def setup_inputs(seed: int = 0, part: int = 0) -> dict:
    streams_of = jax.random.split(jax.random.key(seed), 4)
    part_keys = jax.random.split(jax.random.fold_in(streams_of[3], part), 4)
    spectra = draw_spectra(jax.random.fold_in(jax.random.fold_in(streams_of[3], part), 71), part)
    profiles = scatter_about(streams_of[1], (PROFS, TAPS), TAPS ** -0.5, 0.375)
    shifts = set_ends(jax.random.randint(streams_of[2], (SUBBANDS - 1, 2 * R), 0, MAXSHIFT + 1), jax.random.fold_in(streams_of[2], 1), 0, MAXSHIFT).astype(jnp.int32)
    return dict(spectra=spectra, profiles=profiles, shifts=shifts)


def merge_level(current, shifts, tree_level):
    subband_count, row_count, time_len = current.shape
    device_index = jnp.arange(subband_count, dtype=jnp.int32)
    upper_bit = device_index >> tree_level & 1
    low_index = device_index - upper_bit * (1 << tree_level)
    high_index = low_index + (1 << tree_level)
    tree_node = subband_count - (subband_count >> tree_level) + (device_index >> tree_level + 1)
    merged_row = upper_bit[:, None] * row_count + jnp.arange(row_count, dtype=jnp.int32)[None, :]
    source_row = merged_row // 2
    delays = shifts[tree_node[:, None], merged_row]
    low_rows = current[low_index[:, None], source_row]
    high_rows = current[high_index[:, None], source_row]
    source_time = jnp.arange(time_len, dtype=jnp.int32)[None, None, :] - delays[:, :, None]
    shifted = jnp.take_along_axis(high_rows, jnp.maximum(source_time, 0), axis=2)
    return low_rows + jnp.where(source_time >= 0, shifted, jnp.zeros_like(shifted))

def correlate(rows_bf, profiles, rms_level):
    row_count, time_len = rows_bf.shape
    tap_count = profiles.shape[1]
    positions = time_len // STRIDE
    padded = jnp.pad(rows_bf, ((0, 0), (0, tap_count)))
    frames = padded.reshape(row_count, (time_len + tap_count) // STRIDE, STRIDE)
    windows = jnp.concatenate([frames[:, lag_index:lag_index + positions] for lag_index in range(tap_count // STRIDE)], axis=2)
    products = jnp.einsum('npq,kq->nkp', windows.astype(jnp.float32), profiles.astype(jnp.float32))
    scaled = products / rms_level
    return lax.optimization_barrier(jnp.max(scaled.reshape(row_count, profiles.shape[0], positions // HOLD, HOLD), axis=3)).astype(jnp.bfloat16)

def reference(spectra, profiles, shifts):
    level_count = SUBBANDS.bit_length() - 1
    rms_level = jnp.sqrt(SUBBANDS * jnp.sum(spectra * spectra) / (SUBBANDS * R * TIME) + 1e-06)
    current = spectra.reshape(SUBBANDS, R, TIME)
    for tree_level in range(level_count):
        current = merge_level(current, shifts, tree_level)
    rows_bf = current.astype(jnp.bfloat16)
    peaks_all = lax.map(lambda row_block: correlate(row_block, profiles, rms_level), rows_bf)
    return peaks_all.reshape(SUBBANDS * R, PROFS, PEAKS)
```

```python
import functools

import jax
import jax.numpy as jnp
from jax import lax
from jax.experimental import pallas as pl
from jax.experimental.pallas import tpu as pltpu
from jax.sharding import PartitionSpec as P

STRIDE = 8
HOLD = 16
LANES = STRIDE * HOLD
PAD = 8


def chunk_plan(block_count):
    part = block_count // 4
    sizes = [part + PAD, part, part, part - PAD]
    starts = [sum(sizes[:index]) for index in range(4)]
    return list(zip(starts, sizes)), part


def row_base(device_index, level, level_count, row_bits):
    base = 0
    for place in range(row_bits):
        if level + place < level_count:
            base = base + ((device_index // 2 ** (level + place)) % 2) * 2 ** (row_bits - 1 - place)
    return base


def kernel(
    subbands, chunks, part, spectra_ref, profiles_ref, shifts_ref, out_ref,
    source, table, power_out, power_in, recv0, recv1, recv2, recv3, *rest,
):
    received = (recv0, recv1, recv2, recv3)
    level_count = subbands.bit_length() - 1
    states = rest[: level_count + 1]
    send_sem, recv_sem, power_send, power_recv = rest[level_count + 1 :]
    row_count, time_len = spectra_ref.shape
    row_bits = row_count.bit_length() - 1
    block_count = time_len // LANES
    prof_count, tap_count = profiles_ref.shape
    me = lax.axis_index("freq")

    barrier = pltpu.get_barrier_semaphore()

    def greet(step, carry):
        peer = (me + 1 + step) % subbands
        pl.semaphore_signal(
            barrier, inc=1, device_id={"freq": peer}, device_id_type=pl.DeviceIdType.MESH
        )
        return carry

    lax.fori_loop(0, subbands - 1, greet, 0)

    for state in states:
        state[:, 0:PAD, :] = jnp.zeros((state.shape[0], PAD, LANES), jnp.float32)
    last = states[-1]
    last[:, PAD + block_count :, :] = jnp.zeros((row_count, PAD, LANES), jnp.float32)

    my_row = row_base(me, 0, level_count, row_bits)

    def peer_at(step):
        distance = subbands - 1 - step
        upper = 0
        for bit in range(level_count):
            mine = (me // 2**bit) % 2
            other = (distance // 2**bit) % 2
            upper = upper + ((mine + other) % 2) * 2**bit
        return upper

    power = jnp.zeros((row_count, LANES), jnp.float32)
    for index, (start, size) in enumerate(chunks):
        for block in range(start, start + size):
            piece = spectra_ref[:, block * LANES : (block + 1) * LANES]
            power = power + piece * piece
            source[pl.ds(block, row_count, stride=block_count), :] = piece
        if index == 0:
            pl.semaphore_wait(barrier, subbands - 1)
        inbox = received[index]

        def send(step, carry, inbox=inbox, index=index, start=start, size=size):
            peer = peer_at(step)
            row = row_base(peer, 0, level_count, row_bits)
            first = pl.multiple_of(row * block_count + start, 8)
            pltpu.make_async_remote_copy(
                src_ref=source.at[pl.ds(first, size), :],
                dst_ref=inbox.at[me],
                send_sem=send_sem.at[index],
                recv_sem=recv_sem.at[index],
                device_id={"freq": peer},
                device_id_type=pl.DeviceIdType.MESH,
            ).start()
            return carry

        lax.fori_loop(0, subbands - 1, send, 0)
        mine = pl.multiple_of(my_row * block_count + start, 8)
        inbox[me] = source[pl.ds(mine, size), :]

    power_out[...] = jnp.sum(power, axis=0, keepdims=True)

    def send_power(step, carry):
        peer = peer_at(step)
        pltpu.make_async_remote_copy(
            src_ref=power_out,
            dst_ref=power_in.at[me],
            send_sem=power_send,
            recv_sem=power_recv,
            device_id={"freq": peer},
            device_id_type=pl.DeviceIdType.MESH,
        ).start()
        return carry

    lax.fori_loop(0, subbands - 1, send_power, 0)
    power_in[me] = power_out[...]

    span_len = table.shape[1]
    padded = jnp.concatenate(
        [profiles_ref[...].astype(jnp.float32), jnp.zeros((prof_count, span_len - tap_count), jnp.float32)],
        axis=1,
    )
    for offset in range(HOLD):
        moved = pltpu.roll(padded, offset * STRIDE, 1) if offset else padded
        table[offset * prof_count : (offset + 1) * prof_count, :] = moved.astype(jnp.bfloat16)

    lane = lax.broadcasted_iota(jnp.int32, (1, LANES), 1)
    others = subbands - 1

    def wait_for(ref, sem):
        view = ref.at[pl.ds(0, others)]
        pltpu.make_async_copy(view, view, sem).wait()

    rms_level = None
    for index, (start, size) in enumerate(chunks):
        inbox = received[index]
        wait_for(inbox, recv_sem.at[index])
        if index == 0:
            wait_for(power_in, power_recv)
            total = jnp.sum(jnp.sum(power_in[...], axis=0), axis=1, keepdims=True)
            rms_level = jnp.sqrt(
                subbands * total / (subbands * row_count * time_len) + 1e-06
            )
        rows = pl.ds(PAD + start, size)
        for pair in range(subbands // 2):
            states[0][pair, rows, :] = inbox[2 * pair + 1]
        for level in range(level_count):
            free = max(0, level + 1 - (level_count - row_bits))
            width = 2**free
            above = 2 ** max(0, level - (level_count - row_bits))
            base = ((me // 2**level) % 2) * row_count + row_base(
                me, level + 1, level_count, row_bits
            )
            for group in range(subbands >> (level + 1)):
                node = subbands - (subbands >> level) + group
                for row in range(width):
                    parent = row // 2 if free else 0
                    delay = shifts_ref[node, base + row]
                    whole, rest_len = delay // LANES, delay % LANES
                    if level == 0:
                        low = inbox[2 * group]
                        high_index = group
                    else:
                        low = states[level][2 * group * above + parent, rows, :]
                        high_index = (2 * group + 1) * above + parent
                    near = states[level][high_index, pl.ds(PAD + start - whole, size), :]
                    far = states[level][high_index, pl.ds(PAD - 1 + start - whole, size), :]
                    mixed = jnp.where(lane < LANES - rest_len, near, far)
                    states[level + 1][group * width + row, rows, :] = low + pltpu.roll(mixed, rest_len, 1)
        first = PAD + index * part
        pieces = [
            last[:, first + extra : first + extra + part, :]
            .reshape(row_count * part, LANES)
            .astype(jnp.bfloat16)
            for extra in range(span_len // LANES)
        ]
        windows = jnp.concatenate(pieces, axis=1)
        best = None
        group_rows = 4 * prof_count
        for quarter in range(HOLD // 4):
            product = lax.dot_general(
                table[quarter * group_rows : (quarter + 1) * group_rows, :],
                windows,
                (((1,), (1,)), ((), ())),
                preferred_element_type=jnp.float32,
            )
            top = jnp.max(product.reshape(4, prof_count, row_count * part), axis=0)
            best = top if best is None else jnp.maximum(best, top)
        scaled = best / rms_level
        for row in range(row_count):
            out_ref[row, :, index * part : (index + 1) * part] = scaled[:, row * part : (row + 1) * part]

    for index in range(len(chunks)):
        wait_for(received[index], send_sem.at[index])
    wait_for(power_in, power_send)


def per_device(spectra, profiles, shifts):
    row_count, time_len = spectra.shape
    prof_count, tap_count = profiles.shape
    subbands = lax.axis_size("freq")
    level_count = subbands.bit_length() - 1
    row_bits = row_count.bit_length() - 1
    block_count = time_len // LANES
    chunks, part = chunk_plan(block_count)
    extra = (tap_count + LANES - STRIDE - 1) // LANES
    span_len = (extra + 1) * LANES
    counts = [subbands // 2]
    for level in range(1, level_count + 1):
        counts.append((subbands >> level) * 2 ** max(0, level - (level_count - row_bits)))
    states = [
        pltpu.VMEM((count, block_count + PAD + (PAD if index == level_count else 0), LANES), jnp.float32)
        for index, count in enumerate(counts)
    ]
    peaks = pl.pallas_call(
        functools.partial(kernel, subbands, chunks, part),
        out_shape=jax.ShapeDtypeStruct((row_count, prof_count, block_count), jnp.float32),
        in_specs=[
            pl.BlockSpec(memory_space=pltpu.VMEM),
            pl.BlockSpec(memory_space=pltpu.VMEM),
            pl.BlockSpec(memory_space=pltpu.SMEM),
        ],
        out_specs=pl.BlockSpec(memory_space=pltpu.VMEM),
        scratch_shapes=[
            pltpu.VMEM((row_count * block_count, LANES), jnp.float32),
            pltpu.VMEM((HOLD * prof_count, span_len), jnp.bfloat16),
            pltpu.VMEM((1, LANES), jnp.float32),
            pltpu.VMEM((subbands, 1, LANES), jnp.float32),
            *[pltpu.VMEM((subbands, size, LANES), jnp.float32) for _, size in chunks],
            *states,
            pltpu.SemaphoreType.DMA((len(chunks),)),
            pltpu.SemaphoreType.DMA((len(chunks),)),
            pltpu.SemaphoreType.DMA,
            pltpu.SemaphoreType.DMA,
        ],
        compiler_params=pltpu.CompilerParams(
            collective_id=0, has_side_effects=True, vmem_limit_bytes=40 * 2**20
        ),
        name="merge_and_correlate",
    )(spectra, profiles, shifts)
    return peaks.astype(jnp.bfloat16)


def solution(mesh):
    in_specs = (P(("beam", "freq"), None), P(), P())
    out_specs = P(("beam", "freq"), None, None)
    return jax.shard_map(
        per_device, mesh=mesh, in_specs=in_specs, out_specs=out_specs, check_vma=False
    )
```

```python
import functools

import jax
import jax.numpy as jnp
from jax import lax
from jax.experimental import pallas as pl
from jax.experimental.pallas import tpu as pltpu
from jax.sharding import PartitionSpec as P

STRIDE = 8
HOLD = 16
LANES = STRIDE * HOLD
PAD = 8


def chunk_plan(block_count):
    part = block_count // 4
    sizes = [part + PAD, part, part, part - PAD]
    starts = [sum(sizes[:index]) for index in range(4)]
    return list(zip(starts, sizes)), part


def row_base(device_index, level, level_count, row_bits):
    base = 0
    for place in range(row_bits):
        if level + place < level_count:
            base = base + ((device_index // 2 ** (level + place)) % 2) * 2 ** (row_bits - 1 - place)
    return base


def kernel(
    subbands, chunks, part, spectra_hbm, profiles_hbm, shifts_hbm, out_ref,
    spectra_ref, profiles_ref, shifts_ref, load_sem, source, table, power_out, power_in, recv0, recv1, recv2, recv3, *rest,
):
    received = (recv0, recv1, recv2, recv3)
    level_count = subbands.bit_length() - 1
    states = rest[: level_count + 1]
    send_sem, recv_sem, power_send, power_recv = rest[level_count + 1 :]
    row_count, time_len = spectra_ref.shape
    row_bits = row_count.bit_length() - 1
    block_count = time_len // LANES
    prof_count, tap_count = profiles_ref.shape
    me = lax.axis_index("freq")

    barrier = pltpu.get_barrier_semaphore()

    def greet(step, carry):
        peer = (me + 1 + step) % subbands
        pl.semaphore_signal(
            barrier, inc=1, device_id={"freq": peer}, device_id_type=pl.DeviceIdType.MESH
        )
        return carry

    loads = [
        pltpu.make_async_copy(
            spectra_hbm.at[:, pl.ds(start * LANES, size * LANES)],
            spectra_ref.at[:, pl.ds(start * LANES, size * LANES)],
            load_sem.at[index],
        )
        for index, (start, size) in enumerate(chunks)
    ]
    loads.append(pltpu.make_async_copy(profiles_hbm, profiles_ref, load_sem.at[len(chunks)]))
    loads.append(pltpu.make_async_copy(shifts_hbm, shifts_ref, load_sem.at[len(chunks) + 1]))
    for load in loads:
        load.start()

    lax.fori_loop(0, subbands - 1, greet, 0)

    for state in states:
        state[:, 0:PAD, :] = jnp.zeros((state.shape[0], PAD, LANES), jnp.float32)
    last = states[-1]
    last[:, PAD + block_count :, :] = jnp.zeros((row_count, PAD, LANES), jnp.float32)

    my_row = row_base(me, 0, level_count, row_bits)

    flips = [1 - 2 * ((me // 2**bit) % 2) for bit in range(level_count)]

    def peer_at(distance):
        peer, row = me, my_row
        for bit in range(level_count):
            differs = (distance // 2**bit) % 2
            if isinstance(differs, int) and not differs:
                continue
            peer = peer + differs * 2**bit * flips[bit]
            if bit < row_bits:
                row = row + differs * 2 ** (row_bits - 1 - bit) * flips[bit]
        return peer, row

    def for_peers(send):
        half = subbands // 2

        def step(near, carry):
            send(half + near)
            send(near)
            return carry

        send(half)
        if subbands <= 16:
            for near in range(1, half):
                step(near, 0)
        else:
            lax.fori_loop(1, half, step, 0)

    power = jnp.zeros((row_count, LANES), jnp.float32)
    for index, (start, size) in enumerate(chunks):
        loads[index].wait()
        for block in range(start, start + size):
            piece = spectra_ref[:, block * LANES : (block + 1) * LANES]
            power = power + piece * piece
            source[pl.ds(block, row_count, stride=block_count), :] = piece
        if index == 0:
            pl.semaphore_wait(barrier, subbands - 1)
        inbox = received[index]

        def send(distance, inbox=inbox, index=index, start=start, size=size):
            peer, row = peer_at(distance)
            first = pl.multiple_of(row * block_count + start, 8)
            pltpu.make_async_remote_copy(
                src_ref=source.at[pl.ds(first, size), :],
                dst_ref=inbox.at[me],
                send_sem=send_sem.at[index],
                recv_sem=recv_sem.at[index],
                device_id={"freq": peer},
                device_id_type=pl.DeviceIdType.MESH,
            ).start()

        for_peers(send)
        mine = pl.multiple_of(my_row * block_count + start, 8)
        inbox[me] = source[pl.ds(mine, size), :]

    power_out[...] = jnp.sum(power, axis=0, keepdims=True)

    def send_power(distance):
        peer, _ = peer_at(distance)
        pltpu.make_async_remote_copy(
            src_ref=power_out,
            dst_ref=power_in.at[me],
            send_sem=power_send,
            recv_sem=power_recv,
            device_id={"freq": peer},
            device_id_type=pl.DeviceIdType.MESH,
        ).start()

    for_peers(send_power)
    power_in[me] = power_out[...]

    loads[len(chunks)].wait()
    span_len = table.shape[1]
    padded = jnp.concatenate(
        [profiles_ref[...].astype(jnp.float32), jnp.zeros((prof_count, span_len - tap_count), jnp.float32)],
        axis=1,
    )
    for offset in range(HOLD):
        moved = pltpu.roll(padded, offset * STRIDE, 1) if offset else padded
        table[offset * prof_count : (offset + 1) * prof_count, :] = moved.astype(jnp.bfloat16)

    lane = lax.broadcasted_iota(jnp.int32, (1, LANES), 1)
    others = subbands - 1

    def wait_for(ref, sem):
        view = ref.at[pl.ds(0, others)]
        pltpu.make_async_copy(view, view, sem).wait()

    loads[len(chunks) + 1].wait()
    rms_level = None
    for index, (start, size) in enumerate(chunks):
        inbox = received[index]
        wait_for(inbox, recv_sem.at[index])
        if index == 0:
            wait_for(power_in, power_recv)
            total = jnp.sum(jnp.sum(power_in[...], axis=0), axis=1, keepdims=True)
            rms_level = jnp.sqrt(
                subbands * total / (subbands * row_count * time_len) + 1e-06
            )
        rows = pl.ds(PAD + start, size)
        for pair in range(subbands // 2):
            states[0][pair, rows, :] = inbox[2 * pair + 1]
        for level in range(level_count):
            free = max(0, level + 1 - (level_count - row_bits))
            width = 2**free
            above = 2 ** max(0, level - (level_count - row_bits))
            base = ((me // 2**level) % 2) * row_count + row_base(
                me, level + 1, level_count, row_bits
            )
            for group in range(subbands >> (level + 1)):
                node = subbands - (subbands >> level) + group
                for row in range(width):
                    parent = row // 2 if free else 0
                    delay = shifts_ref[node, base + row]
                    whole, rest_len = delay // LANES, delay % LANES
                    if level == 0:
                        low = inbox[2 * group]
                        high_index = group
                    else:
                        low = states[level][2 * group * above + parent, rows, :]
                        high_index = (2 * group + 1) * above + parent
                    near = states[level][high_index, pl.ds(PAD + start - whole, size), :]
                    far = states[level][high_index, pl.ds(PAD - 1 + start - whole, size), :]
                    mixed = jnp.where(lane < LANES - rest_len, near, far)
                    states[level + 1][group * width + row, rows, :] = low + pltpu.roll(mixed, rest_len, 1)
        first = PAD + index * part
        pieces = [
            last[:, first + extra : first + extra + part, :]
            .reshape(row_count * part, LANES)
            .astype(jnp.bfloat16)
            for extra in range(span_len // LANES)
        ]
        windows = jnp.concatenate(pieces, axis=1)
        best = None
        group_rows = 4 * prof_count
        for quarter in range(HOLD // 4):
            product = lax.dot_general(
                table[quarter * group_rows : (quarter + 1) * group_rows, :],
                windows,
                (((1,), (1,)), ((), ())),
                preferred_element_type=jnp.float32,
            )
            top = jnp.max(product.reshape(4, prof_count, row_count * part), axis=0)
            best = top if best is None else jnp.maximum(best, top)
        scaled = best / rms_level
        for row in range(row_count):
            out_ref[row, :, index * part : (index + 1) * part] = scaled[:, row * part : (row + 1) * part]

    for index in range(len(chunks)):
        wait_for(received[index], send_sem.at[index])
    wait_for(power_in, power_send)


def per_device(spectra, profiles, shifts):
    row_count, time_len = spectra.shape
    prof_count, tap_count = profiles.shape
    subbands = lax.axis_size("freq")
    level_count = subbands.bit_length() - 1
    row_bits = row_count.bit_length() - 1
    block_count = time_len // LANES
    chunks, part = chunk_plan(block_count)
    extra = (tap_count + LANES - STRIDE - 1) // LANES
    span_len = (extra + 1) * LANES
    counts = [subbands // 2]
    for level in range(1, level_count + 1):
        counts.append((subbands >> level) * 2 ** max(0, level - (level_count - row_bits)))
    states = [
        pltpu.VMEM((count, block_count + PAD + (PAD if index == level_count else 0), LANES), jnp.float32)
        for index, count in enumerate(counts)
    ]
    peaks = pl.pallas_call(
        functools.partial(kernel, subbands, chunks, part),
        out_shape=jax.ShapeDtypeStruct((row_count, prof_count, block_count), jnp.float32),
        in_specs=[
            pl.BlockSpec(memory_space=pltpu.HBM),
            pl.BlockSpec(memory_space=pltpu.HBM),
            pl.BlockSpec(memory_space=pltpu.HBM),
        ],
        out_specs=pl.BlockSpec(memory_space=pltpu.VMEM),
        scratch_shapes=[
            pltpu.VMEM(spectra.shape, spectra.dtype),
            pltpu.VMEM(profiles.shape, profiles.dtype),
            pltpu.SMEM(shifts.shape, shifts.dtype),
            pltpu.SemaphoreType.DMA((len(chunks) + 2,)),
            pltpu.VMEM((row_count * block_count, LANES), jnp.float32),
            pltpu.VMEM((HOLD * prof_count, span_len), jnp.bfloat16),
            pltpu.VMEM((1, LANES), jnp.float32),
            pltpu.VMEM((subbands, 1, LANES), jnp.float32),
            *[pltpu.VMEM((subbands, size, LANES), jnp.float32) for _, size in chunks],
            *states,
            pltpu.SemaphoreType.DMA((len(chunks),)),
            pltpu.SemaphoreType.DMA((len(chunks),)),
            pltpu.SemaphoreType.DMA,
            pltpu.SemaphoreType.DMA,
        ],
        compiler_params=pltpu.CompilerParams(
            collective_id=0, has_side_effects=True, vmem_limit_bytes=64 * 2**20
        ),
        name="merge_and_correlate",
    )(spectra, profiles, shifts)
    return peaks.astype(jnp.bfloat16)


def solution(mesh):
    in_specs = (P(("beam", "freq"), None), P(), P())
    out_specs = P(("beam", "freq"), None, None)
    return jax.shard_map(
        per_device, mesh=mesh, in_specs=in_specs, out_specs=out_specs, check_vma=False
    )
```

```python
import functools

import jax
import jax.numpy as jnp
from jax import lax
from jax.experimental import pallas as pl
from jax.experimental.pallas import tpu as pltpu
from jax.sharding import PartitionSpec as P

STRIDE = 8
HOLD = 16
LANES = STRIDE * HOLD
PAD = 8


def chunk_plan(block_count):
    part = block_count // 4
    sizes = [part + PAD, part, part, part - PAD]
    starts = [sum(sizes[:index]) for index in range(4)]
    return list(zip(starts, sizes)), part


def row_base(device_index, level, level_count, row_bits):
    base = 0
    for place in range(row_bits):
        if level + place < level_count:
            base = base + ((device_index // 2 ** (level + place)) % 2) * 2 ** (row_bits - 1 - place)
    return base


def kernel(
    subbands, chunks, part, spectra_hbm, profiles_hbm, shifts_hbm, out_ref,
    spectra_ref, profiles_ref, shifts_ref, load_sem, source, table, power_out, power_in, recv0, recv1, recv2, recv3, *rest,
):
    received = (recv0, recv1, recv2, recv3)
    level_count = subbands.bit_length() - 1
    states = rest[: level_count + 1]
    send_sem, recv_sem, power_send, power_recv = rest[level_count + 1 :]
    row_count, time_len = spectra_ref.shape
    row_bits = row_count.bit_length() - 1
    block_count = time_len // LANES
    prof_count, tap_count = profiles_ref.shape
    me = lax.axis_index("freq")

    barrier = pltpu.get_barrier_semaphore()

    def greet(step, carry):
        peer = (me + 1 + step) % subbands
        pl.semaphore_signal(
            barrier, inc=1, device_id={"freq": peer}, device_id_type=pl.DeviceIdType.MESH
        )
        return carry

    loads = [
        pltpu.make_async_copy(
            spectra_hbm.at[:, pl.ds(start * LANES, size * LANES)],
            spectra_ref.at[:, pl.ds(start * LANES, size * LANES)],
            load_sem.at[index],
        )
        for index, (start, size) in enumerate(chunks)
    ]
    loads.append(pltpu.make_async_copy(profiles_hbm, profiles_ref, load_sem.at[len(chunks)]))
    loads.append(pltpu.make_async_copy(shifts_hbm, shifts_ref, load_sem.at[len(chunks) + 1]))
    for load in loads:
        load.start()

    lax.fori_loop(0, subbands - 1, greet, 0)

    for state in states:
        state[:, 0:PAD, :] = jnp.zeros((state.shape[0], PAD, LANES), jnp.float32)
    last = states[-1]
    last[:, PAD + block_count :, :] = jnp.zeros((row_count, PAD, LANES), jnp.float32)

    my_row = row_base(me, 0, level_count, row_bits)

    flips = [1 - 2 * ((me // 2**bit) % 2) for bit in range(level_count)]

    def peer_at(distance):
        peer, row = me, my_row
        for bit in range(level_count):
            differs = (distance // 2**bit) % 2
            if isinstance(differs, int) and not differs:
                continue
            peer = peer + differs * 2**bit * flips[bit]
            if bit < row_bits:
                row = row + differs * 2 ** (row_bits - 1 - bit) * flips[bit]
        return peer, row

    def for_peers(send):
        half = subbands // 2

        def step(near, carry):
            send(half + near)
            send(near)
            return carry

        send(half)
        if subbands <= 16:
            for near in range(1, half):
                step(near, 0)
        else:
            lax.fori_loop(1, half, step, 0)

    total_power = [jnp.zeros((row_count, LANES), jnp.float32)]

    def send_chunk(index):
        start, size = chunks[index]
        inbox = received[index]
        if index < 2:
            loads[index].wait()
        power = total_power[0]
        for block in range(start, start + size):
            piece = spectra_ref[:, block * LANES : (block + 1) * LANES]
            if index < 2:
                power = power + piece * piece
            source[pl.ds(block, row_count, stride=block_count), :] = piece
        total_power[0] = power
        if index == 0:
            pl.semaphore_wait(barrier, subbands - 1)

        def send(distance):
            peer, row = peer_at(distance)
            first = pl.multiple_of(row * block_count + start, 8)
            pltpu.make_async_remote_copy(
                src_ref=source.at[pl.ds(first, size), :],
                dst_ref=inbox.at[me],
                send_sem=send_sem.at[index],
                recv_sem=recv_sem.at[index],
                device_id={"freq": peer},
                device_id_type=pl.DeviceIdType.MESH,
            ).start()

        for_peers(send)
        mine = pl.multiple_of(my_row * block_count + start, 8)
        inbox[me] = source[pl.ds(mine, size), :]

    send_chunk(0)
    send_chunk(1)
    for index in range(2, len(chunks)):
        start, size = chunks[index]
        loads[index].wait()
        for block in range(start, start + size):
            piece = spectra_ref[:, block * LANES : (block + 1) * LANES]
            total_power[0] = total_power[0] + piece * piece
    power = total_power[0]
    power_out[...] = jnp.sum(power, axis=0, keepdims=True)

    def send_power(distance):
        peer, _ = peer_at(distance)
        pltpu.make_async_remote_copy(
            src_ref=power_out,
            dst_ref=power_in.at[me],
            send_sem=power_send,
            recv_sem=power_recv,
            device_id={"freq": peer},
            device_id_type=pl.DeviceIdType.MESH,
        ).start()

    for_peers(send_power)
    power_in[me] = power_out[...]

    loads[len(chunks)].wait()
    span_len = table.shape[1]
    padded = jnp.concatenate(
        [profiles_ref[...].astype(jnp.float32), jnp.zeros((prof_count, span_len - tap_count), jnp.float32)],
        axis=1,
    )
    for offset in range(HOLD):
        moved = pltpu.roll(padded, offset * STRIDE, 1) if offset else padded
        table[offset * prof_count : (offset + 1) * prof_count, :] = moved.astype(jnp.bfloat16)

    lane = lax.broadcasted_iota(jnp.int32, (1, LANES), 1)
    others = subbands - 1
    lane_bits = LANES.bit_length() - 1

    def wait_for(ref, sem):
        view = ref.at[pl.ds(0, others)]
        pltpu.make_async_copy(view, view, sem).wait()

    loads[len(chunks) + 1].wait()
    rms_level = None
    for index, (start, size) in enumerate(chunks):
        inbox = received[index]
        wait_for(inbox, recv_sem.at[index])
        if index + 2 < len(chunks):
            send_chunk(index + 2)
        if index == 0:
            wait_for(power_in, power_recv)
            total = jnp.sum(jnp.sum(power_in[...], axis=0), axis=1, keepdims=True)
            rms_level = jnp.sqrt(
                subbands * total / (subbands * row_count * time_len) + 1e-06
            )
        rows = pl.ds(PAD + start, size)
        for pair in range(subbands // 2):
            states[0][pair, rows, :] = inbox[2 * pair + 1]
        for level in range(level_count):
            free = max(0, level + 1 - (level_count - row_bits))
            width = 2**free
            above = 2 ** max(0, level - (level_count - row_bits))
            base = ((me // 2**level) % 2) * row_count + row_base(
                me, level + 1, level_count, row_bits
            )
            for group in range(subbands >> (level + 1)):
                node = subbands - (subbands >> level) + group
                for row in range(width):
                    parent = row // 2 if free else 0
                    delay = shifts_ref[node, base + row]
                    whole, rest_len = delay >> lane_bits, delay & (LANES - 1)
                    if level == 0:
                        low = inbox[2 * group]
                        high_index = group
                    else:
                        low = states[level][2 * group * above + parent, rows, :]
                        high_index = (2 * group + 1) * above + parent
                    near = states[level][high_index, pl.ds(PAD + start - whole, size), :]
                    far = states[level][high_index, pl.ds(PAD - 1 + start - whole, size), :]
                    mixed = jnp.where(lane < LANES - rest_len, near, far)
                    states[level + 1][group * width + row, rows, :] = low + pltpu.roll(mixed, rest_len, 1)
        first = PAD + index * part
        pieces = [
            last[:, first + extra : first + extra + part, :]
            .reshape(row_count * part, LANES)
            .astype(jnp.bfloat16)
            for extra in range(span_len // LANES)
        ]
        windows = jnp.concatenate(pieces, axis=1)
        best = None
        group_rows = 4 * prof_count
        for quarter in range(HOLD // 4):
            product = lax.dot_general(
                table[quarter * group_rows : (quarter + 1) * group_rows, :],
                windows,
                (((1,), (1,)), ((), ())),
                preferred_element_type=jnp.float32,
            )
            top = jnp.max(product.reshape(4, prof_count, row_count * part), axis=0)
            best = top if best is None else jnp.maximum(best, top)
        scaled = (best / rms_level).astype(jnp.bfloat16)
        for row in range(row_count):
            out_ref[row, :, index * part : (index + 1) * part] = scaled[:, row * part : (row + 1) * part]

    for index in range(len(chunks)):
        wait_for(received[index], send_sem.at[index])
    wait_for(power_in, power_send)


def per_device(spectra, profiles, shifts):
    row_count, time_len = spectra.shape
    prof_count, tap_count = profiles.shape
    subbands = lax.axis_size("freq")
    level_count = subbands.bit_length() - 1
    row_bits = row_count.bit_length() - 1
    block_count = time_len // LANES
    chunks, part = chunk_plan(block_count)
    extra = (tap_count + LANES - STRIDE - 1) // LANES
    span_len = (extra + 1) * LANES
    counts = [subbands // 2]
    for level in range(1, level_count + 1):
        counts.append((subbands >> level) * 2 ** max(0, level - (level_count - row_bits)))
    states = [
        pltpu.VMEM((count, block_count + PAD + (PAD if index == level_count else 0), LANES), jnp.float32)
        for index, count in enumerate(counts)
    ]
    peaks = pl.pallas_call(
        functools.partial(kernel, subbands, chunks, part),
        out_shape=jax.ShapeDtypeStruct((row_count, prof_count, block_count), jnp.bfloat16),
        in_specs=[
            pl.BlockSpec(memory_space=pltpu.HBM),
            pl.BlockSpec(memory_space=pltpu.HBM),
            pl.BlockSpec(memory_space=pltpu.HBM),
        ],
        out_specs=pl.BlockSpec(memory_space=pltpu.VMEM),
        scratch_shapes=[
            pltpu.VMEM(spectra.shape, spectra.dtype),
            pltpu.VMEM(profiles.shape, profiles.dtype),
            pltpu.SMEM(shifts.shape, shifts.dtype),
            pltpu.SemaphoreType.DMA((len(chunks) + 2,)),
            pltpu.VMEM((row_count * block_count, LANES), jnp.float32),
            pltpu.VMEM((HOLD * prof_count, span_len), jnp.bfloat16),
            pltpu.VMEM((1, LANES), jnp.float32),
            pltpu.VMEM((subbands, 1, LANES), jnp.float32),
            *[pltpu.VMEM((subbands, size, LANES), jnp.float32) for _, size in chunks],
            *states,
            pltpu.SemaphoreType.DMA((len(chunks),)),
            pltpu.SemaphoreType.DMA((len(chunks),)),
            pltpu.SemaphoreType.DMA,
            pltpu.SemaphoreType.DMA,
        ],
        compiler_params=pltpu.CompilerParams(
            collective_id=0, has_side_effects=True, vmem_limit_bytes=64 * 2**20 - 272 * 2**10
        ),
        name="merge_and_correlate",
    )(spectra, profiles, shifts)
    return peaks


def solution(mesh):
    in_specs = (P(("beam", "freq"), None), P(), P())
    out_specs = P(("beam", "freq"), None, None)
    return jax.shard_map(
        per_device, mesh=mesh, in_specs=in_specs, out_specs=out_specs, check_vma=False
    )
```

```python
import functools

import jax
import jax.numpy as jnp
from jax import lax
from jax.experimental import pallas as pl
from jax.experimental.pallas import tpu as pltpu
from jax.sharding import PartitionSpec as P

STRIDE = 8
HOLD = 16
LANES = STRIDE * HOLD
PAD = 8


PARTS = 2


def chunk_plan(block_count):
    part = block_count // PARTS
    sizes = [part + PAD] + [part] * (PARTS - 2) + [part - PAD]
    starts = [sum(sizes[:index]) for index in range(PARTS)]
    return list(zip(starts, sizes)), part


def row_base(device_index, level, level_count, row_bits):
    base = 0
    for place in range(row_bits):
        if level + place < level_count:
            base = base + ((device_index // 2 ** (level + place)) % 2) * 2 ** (row_bits - 1 - place)
    return base


def kernel(
    subbands, chunks, part, spectra_hbm, profiles_hbm, shifts_hbm, out_ref,
    spectra_ref, profiles_ref, shifts_ref, load_sem, source, table, power_out, power_in, *rest,
):
    received, rest = rest[: len(chunks)], rest[len(chunks) :]
    level_count = subbands.bit_length() - 1
    states = rest[: level_count + 1]
    send_sem, recv_sem, power_send, power_recv = rest[level_count + 1 :]
    row_count, time_len = spectra_ref.shape
    row_bits = row_count.bit_length() - 1
    block_count = time_len // LANES
    prof_count, tap_count = profiles_ref.shape
    me = lax.axis_index("freq")

    barrier = pltpu.get_barrier_semaphore()

    def greet(step, carry):
        peer = (me + 1 + step) % subbands
        pl.semaphore_signal(
            barrier, inc=1, device_id={"freq": peer}, device_id_type=pl.DeviceIdType.MESH
        )
        return carry

    loads = [
        pltpu.make_async_copy(
            spectra_hbm.at[:, pl.ds(start * LANES, size * LANES)],
            spectra_ref.at[:, pl.ds(start * LANES, size * LANES)],
            load_sem.at[index],
        )
        for index, (start, size) in enumerate(chunks)
    ]
    loads.append(pltpu.make_async_copy(profiles_hbm, profiles_ref, load_sem.at[len(chunks)]))
    loads.append(pltpu.make_async_copy(shifts_hbm, shifts_ref, load_sem.at[len(chunks) + 1]))
    for load in loads:
        load.start()

    lax.fori_loop(0, subbands - 1, greet, 0)

    for state in states:
        state[:, 0:PAD, :] = jnp.zeros((state.shape[0], PAD, LANES), jnp.float32)
    last = states[-1]
    last[:, PAD + block_count :, :] = jnp.zeros((row_count, PAD, LANES), jnp.float32)

    my_row = row_base(me, 0, level_count, row_bits)

    flips = [1 - 2 * ((me // 2**bit) % 2) for bit in range(level_count)]

    def peer_at(distance):
        peer, row = me, my_row
        for bit in range(level_count):
            differs = (distance // 2**bit) % 2
            if isinstance(differs, int) and not differs:
                continue
            peer = peer + differs * 2**bit * flips[bit]
            if bit < row_bits:
                row = row + differs * 2 ** (row_bits - 1 - bit) * flips[bit]
        return peer, row

    def for_peers(send):
        half = subbands // 2

        def step(near, carry):
            send(half + near)
            send(near)
            return carry

        send(half)
        if subbands <= 16:
            for near in range(1, half):
                step(near, 0)
        else:
            lax.fori_loop(1, half, step, 0)

    total_power = [jnp.zeros((row_count, LANES), jnp.float32)]

    def send_chunk(index):
        start, size = chunks[index]
        inbox = received[index]
        loads[index].wait()
        power = total_power[0]
        for block in range(start, start + size):
            piece = spectra_ref[:, block * LANES : (block + 1) * LANES]
            power = power + piece * piece
            source[pl.ds(block, row_count, stride=block_count), :] = piece
        total_power[0] = power
        if index == 0:
            pl.semaphore_wait(barrier, subbands - 1)

        def send(distance):
            peer, row = peer_at(distance)
            first = pl.multiple_of(row * block_count + start, 8)
            pltpu.make_async_remote_copy(
                src_ref=source.at[pl.ds(first, size), :],
                dst_ref=inbox.at[me],
                send_sem=send_sem.at[index],
                recv_sem=recv_sem.at[index],
                device_id={"freq": peer},
                device_id_type=pl.DeviceIdType.MESH,
            ).start()

        for_peers(send)
        mine = pl.multiple_of(my_row * block_count + start, 8)
        inbox[me] = source[pl.ds(mine, size), :]

    for index in range(len(chunks)):
        send_chunk(index)
    power = total_power[0]
    power_out[...] = jnp.sum(power, axis=0, keepdims=True)

    def send_power(distance):
        peer, _ = peer_at(distance)
        pltpu.make_async_remote_copy(
            src_ref=power_out,
            dst_ref=power_in.at[me],
            send_sem=power_send,
            recv_sem=power_recv,
            device_id={"freq": peer},
            device_id_type=pl.DeviceIdType.MESH,
        ).start()

    for_peers(send_power)
    power_in[me] = power_out[...]

    loads[len(chunks)].wait()
    span_len = table.shape[1]
    padded = jnp.concatenate(
        [profiles_ref[...].astype(jnp.float32), jnp.zeros((prof_count, span_len - tap_count), jnp.float32)],
        axis=1,
    )
    for offset in range(HOLD):
        moved = pltpu.roll(padded, offset * STRIDE, 1) if offset else padded
        table[offset * prof_count : (offset + 1) * prof_count, :] = moved.astype(jnp.bfloat16)

    lane = lax.broadcasted_iota(jnp.int32, (1, LANES), 1)
    others = subbands - 1
    lane_bits = LANES.bit_length() - 1

    def wait_for(ref, sem):
        view = ref.at[pl.ds(0, others)]
        pltpu.make_async_copy(view, view, sem).wait()

    loads[len(chunks) + 1].wait()
    rms_level = None
    for index, (start, size) in enumerate(chunks):
        inbox = received[index]
        wait_for(inbox, recv_sem.at[index])
        if index == 0:
            wait_for(power_in, power_recv)
            total = jnp.sum(jnp.sum(power_in[...], axis=0), axis=1, keepdims=True)
            rms_level = jnp.sqrt(
                subbands * total / (subbands * row_count * time_len) + 1e-06
            )
        rows = pl.ds(PAD + start, size)
        for pair in range(subbands // 2):
            states[0][pair, rows, :] = inbox[2 * pair + 1]
        for level in range(level_count):
            free = max(0, level + 1 - (level_count - row_bits))
            width = 2**free
            above = 2 ** max(0, level - (level_count - row_bits))
            base = ((me // 2**level) % 2) * row_count + row_base(
                me, level + 1, level_count, row_bits
            )
            for group in range(subbands >> (level + 1)):
                node = subbands - (subbands >> level) + group
                for row in range(width):
                    parent = row // 2 if free else 0
                    delay = shifts_ref[node, base + row]
                    whole, rest_len = delay >> lane_bits, delay & (LANES - 1)
                    if level == 0:
                        low = inbox[2 * group]
                        high_index = group
                    else:
                        low = states[level][2 * group * above + parent, rows, :]
                        high_index = (2 * group + 1) * above + parent
                    near = states[level][high_index, pl.ds(PAD + start - whole, size), :]
                    far = states[level][high_index, pl.ds(PAD - 1 + start - whole, size), :]
                    mixed = jnp.where(lane < LANES - rest_len, near, far)
                    states[level + 1][group * width + row, rows, :] = low + pltpu.roll(mixed, rest_len, 1)
        first = PAD + index * part
        pieces = [
            last[:, first + extra : first + extra + part, :]
            .reshape(row_count * part, LANES)
            .astype(jnp.bfloat16)
            for extra in range(span_len // LANES)
        ]
        windows = jnp.concatenate(pieces, axis=1)
        best = None
        group_rows = 4 * prof_count
        for quarter in range(HOLD // 4):
            product = lax.dot_general(
                table[quarter * group_rows : (quarter + 1) * group_rows, :],
                windows,
                (((1,), (1,)), ((), ())),
                preferred_element_type=jnp.float32,
            )
            top = jnp.max(product.reshape(4, prof_count, row_count * part), axis=0)
            best = top if best is None else jnp.maximum(best, top)
        scaled = (best / rms_level).astype(jnp.bfloat16)
        for row in range(row_count):
            out_ref[row, :, index * part : (index + 1) * part] = scaled[:, row * part : (row + 1) * part]

    for index in range(len(chunks)):
        wait_for(received[index], send_sem.at[index])
    wait_for(power_in, power_send)


def per_device(spectra, profiles, shifts):
    row_count, time_len = spectra.shape
    prof_count, tap_count = profiles.shape
    subbands = lax.axis_size("freq")
    level_count = subbands.bit_length() - 1
    row_bits = row_count.bit_length() - 1
    block_count = time_len // LANES
    chunks, part = chunk_plan(block_count)
    extra = (tap_count + LANES - STRIDE - 1) // LANES
    span_len = (extra + 1) * LANES
    counts = [subbands // 2]
    for level in range(1, level_count + 1):
        counts.append((subbands >> level) * 2 ** max(0, level - (level_count - row_bits)))
    states = [
        pltpu.VMEM((count, block_count + PAD + (PAD if index == level_count else 0), LANES), jnp.float32)
        for index, count in enumerate(counts)
    ]
    peaks = pl.pallas_call(
        functools.partial(kernel, subbands, chunks, part),
        out_shape=jax.ShapeDtypeStruct((row_count, prof_count, block_count), jnp.bfloat16),
        in_specs=[
            pl.BlockSpec(memory_space=pltpu.HBM),
            pl.BlockSpec(memory_space=pltpu.HBM),
            pl.BlockSpec(memory_space=pltpu.HBM),
        ],
        out_specs=pl.BlockSpec(memory_space=pltpu.VMEM),
        scratch_shapes=[
            pltpu.VMEM(spectra.shape, spectra.dtype),
            pltpu.VMEM(profiles.shape, profiles.dtype),
            pltpu.SMEM(shifts.shape, shifts.dtype),
            pltpu.SemaphoreType.DMA((len(chunks) + 2,)),
            pltpu.VMEM((row_count * block_count, LANES), jnp.float32),
            pltpu.VMEM((HOLD * prof_count, span_len), jnp.bfloat16),
            pltpu.VMEM((1, LANES), jnp.float32),
            pltpu.VMEM((subbands, 1, LANES), jnp.float32),
            *[pltpu.VMEM((subbands, size, LANES), jnp.float32) for _, size in chunks],
            *states,
            pltpu.SemaphoreType.DMA((len(chunks),)),
            pltpu.SemaphoreType.DMA((len(chunks),)),
            pltpu.SemaphoreType.DMA,
            pltpu.SemaphoreType.DMA,
        ],
        compiler_params=pltpu.CompilerParams(
            collective_id=0, has_side_effects=True, vmem_limit_bytes=40 * 2**20
        ),
        name="merge_and_correlate",
    )(*[pltpu.with_memory_space_constraint(array, pltpu.HBM) for array in (spectra, profiles, shifts)])
    return peaks


def solution(mesh):
    in_specs = (P(("beam", "freq"), None), P(), P())
    out_specs = P(("beam", "freq"), None, None)
    return jax.shard_map(
        per_device, mesh=mesh, in_specs=in_specs, out_specs=out_specs, check_vma=False
    )
```

```python
import functools

import jax
import jax.numpy as jnp
from jax import lax
from jax.experimental import pallas as pl
from jax.experimental.pallas import tpu as pltpu
from jax.sharding import PartitionSpec as P

STRIDE = 8
HOLD = 16
LANES = STRIDE * HOLD
PAD = 8


TAIL = 16


def chunk_plan(block_count):
    first = block_count - TAIL
    return [(0, first, 0, first - PAD), (first, TAIL, first - PAD, TAIL + PAD)]


def row_base(device_index, level, level_count, row_bits):
    base = 0
    for place in range(row_bits):
        if level + place < level_count:
            base = base + ((device_index // 2 ** (level + place)) % 2) * 2 ** (row_bits - 1 - place)
    return base


def kernel(
    subbands, chunks, spectra_hbm, profiles_hbm, shifts_hbm, out_ref,
    spectra_ref, profiles_ref, shifts_ref, load_sem, source, table, power_out, power_in, *rest,
):
    received, rest = rest[: len(chunks)], rest[len(chunks) :]
    level_count = subbands.bit_length() - 1
    states = rest[: level_count + 1]
    send_sem, recv_sem, power_send, power_recv = rest[level_count + 1 :]
    row_count, time_len = spectra_ref.shape
    row_bits = row_count.bit_length() - 1
    block_count = time_len // LANES
    prof_count, tap_count = profiles_ref.shape
    me = lax.axis_index("freq")

    barrier = pltpu.get_barrier_semaphore()

    def greet(step, carry):
        peer = (me + 1 + step) % subbands
        pl.semaphore_signal(
            barrier, inc=1, device_id={"freq": peer}, device_id_type=pl.DeviceIdType.MESH
        )
        return carry

    loads = [
        pltpu.make_async_copy(
            spectra_hbm.at[:, pl.ds(start * LANES, size * LANES)],
            spectra_ref.at[:, pl.ds(start * LANES, size * LANES)],
            load_sem.at[index],
        )
        for index, (start, size, _, _) in enumerate(chunks)
    ]
    loads.append(pltpu.make_async_copy(profiles_hbm, profiles_ref, load_sem.at[len(chunks)]))
    loads.append(pltpu.make_async_copy(shifts_hbm, shifts_ref, load_sem.at[len(chunks) + 1]))
    for load in loads:
        load.start()

    lax.fori_loop(0, subbands - 1, greet, 0)

    for state in states:
        state[:, 0:PAD, :] = jnp.zeros((state.shape[0], PAD, LANES), jnp.float32)
    last = states[-1]
    last[:, PAD + block_count :, :] = jnp.zeros((row_count, PAD, LANES), jnp.float32)

    my_row = row_base(me, 0, level_count, row_bits)

    flips = [1 - 2 * ((me // 2**bit) % 2) for bit in range(level_count)]

    def peer_at(distance):
        peer, row = me, my_row
        for bit in range(level_count):
            differs = (distance // 2**bit) % 2
            if isinstance(differs, int) and not differs:
                continue
            peer = peer + differs * 2**bit * flips[bit]
            if bit < row_bits:
                row = row + differs * 2 ** (row_bits - 1 - bit) * flips[bit]
        return peer, row

    def for_peers(send):
        half = subbands // 2

        def step(near, carry):
            send(half + near)
            send(near)
            return carry

        send(half)
        if subbands <= 16:
            for near in range(1, half):
                step(near, 0)
        else:
            lax.fori_loop(1, half, step, 0)

    total_power = [jnp.zeros((row_count, LANES), jnp.float32)]

    def lay_out(index):
        start, size, _, _ = chunks[index]
        loads[index].wait()
        power = total_power[0]
        for block in range(start, start + size):
            piece = spectra_ref[:, block * LANES : (block + 1) * LANES]
            power = power + piece * piece
            source[pl.ds(block, row_count, stride=block_count), :] = piece
        total_power[0] = power

    def send_chunk(index):
        start, size, _, _ = chunks[index]
        inbox = received[index]

        def send(distance):
            peer, row = peer_at(distance)
            first = pl.multiple_of(row * block_count + start, 8)
            pltpu.make_async_remote_copy(
                src_ref=source.at[pl.ds(first, size), :],
                dst_ref=inbox.at[me],
                send_sem=send_sem.at[index],
                recv_sem=recv_sem.at[index],
                device_id={"freq": peer},
                device_id_type=pl.DeviceIdType.MESH,
            ).start()

        for_peers(send)
        mine = pl.multiple_of(my_row * block_count + start, 8)
        inbox[me] = source[pl.ds(mine, size), :]

    def send_power(distance):
        peer, _ = peer_at(distance)
        pltpu.make_async_remote_copy(
            src_ref=power_out,
            dst_ref=power_in.at[me],
            send_sem=power_send,
            recv_sem=power_recv,
            device_id={"freq": peer},
            device_id_type=pl.DeviceIdType.MESH,
        ).start()

    lay_out(0)
    pl.semaphore_wait(barrier, subbands - 1)
    send_chunk(0)
    lay_out(1)
    power_out[...] = jnp.sum(total_power[0], axis=0, keepdims=True)
    for_peers(send_power)
    power_in[me] = power_out[...]
    send_chunk(1)

    loads[len(chunks)].wait()
    span_len = table.shape[1]
    padded = jnp.concatenate(
        [profiles_ref[...].astype(jnp.float32), jnp.zeros((prof_count, span_len - tap_count), jnp.float32)],
        axis=1,
    )
    for offset in range(HOLD):
        moved = pltpu.roll(padded, offset * STRIDE, 1) if offset else padded
        table[offset * prof_count : (offset + 1) * prof_count, :] = moved.astype(jnp.bfloat16)

    lane = lax.broadcasted_iota(jnp.int32, (1, LANES), 1)
    others = subbands - 1
    lane_bits = LANES.bit_length() - 1

    def wait_for(ref, sem):
        view = ref.at[pl.ds(0, others)]
        pltpu.make_async_copy(view, view, sem).wait()

    loads[len(chunks) + 1].wait()
    rms_level = None
    for index, (start, size, place, part) in enumerate(chunks):
        inbox = received[index]
        wait_for(inbox, recv_sem.at[index])
        rows = pl.ds(PAD + start, size)
        for pair in range(subbands // 2):
            states[0][pair, rows, :] = inbox[2 * pair + 1]
        for level in range(level_count):
            free = max(0, level + 1 - (level_count - row_bits))
            width = 2**free
            above = 2 ** max(0, level - (level_count - row_bits))
            base = ((me // 2**level) % 2) * row_count + row_base(
                me, level + 1, level_count, row_bits
            )
            for group in range(subbands >> (level + 1)):
                node = subbands - (subbands >> level) + group
                for row in range(width):
                    parent = row // 2 if free else 0
                    delay = shifts_ref[node, base + row]
                    whole, rest_len = delay >> lane_bits, delay & (LANES - 1)
                    if level == 0:
                        low = inbox[2 * group]
                        high_index = group
                    else:
                        low = states[level][2 * group * above + parent, rows, :]
                        high_index = (2 * group + 1) * above + parent
                    near = states[level][high_index, pl.ds(PAD + start - whole, size), :]
                    far = states[level][high_index, pl.ds(PAD - 1 + start - whole, size), :]
                    mixed = jnp.where(lane < LANES - rest_len, near, far)
                    states[level + 1][group * width + row, rows, :] = low + pltpu.roll(mixed, rest_len, 1)
        first = PAD + place
        pieces = [
            last[:, first + extra : first + extra + part, :]
            .reshape(row_count * part, LANES)
            .astype(jnp.bfloat16)
            for extra in range(span_len // LANES)
        ]
        windows = jnp.concatenate(pieces, axis=1)
        best = None
        group_rows = 4 * prof_count
        for quarter in range(HOLD // 4):
            product = lax.dot_general(
                table[quarter * group_rows : (quarter + 1) * group_rows, :],
                windows,
                (((1,), (1,)), ((), ())),
                preferred_element_type=jnp.float32,
            )
            top = jnp.max(product.reshape(4, prof_count, row_count * part), axis=0)
            best = top if best is None else jnp.maximum(best, top)
        if index == 0:
            wait_for(power_in, power_recv)
            total = jnp.sum(jnp.sum(power_in[...], axis=0), axis=1, keepdims=True)
            rms_level = jnp.sqrt(
                subbands * total / (subbands * row_count * time_len) + 1e-06
            )
        scaled = (best / rms_level).astype(jnp.bfloat16)
        for row in range(row_count):
            out_ref[row, :, place : place + part] = scaled[:, row * part : (row + 1) * part]

    for index in range(len(chunks)):
        wait_for(received[index], send_sem.at[index])
    wait_for(power_in, power_send)


def per_device(spectra, profiles, shifts):
    row_count, time_len = spectra.shape
    prof_count, tap_count = profiles.shape
    subbands = lax.axis_size("freq")
    level_count = subbands.bit_length() - 1
    row_bits = row_count.bit_length() - 1
    block_count = time_len // LANES
    chunks = chunk_plan(block_count)
    extra = (tap_count + LANES - STRIDE - 1) // LANES
    span_len = (extra + 1) * LANES
    counts = [subbands // 2]
    for level in range(1, level_count + 1):
        counts.append((subbands >> level) * 2 ** max(0, level - (level_count - row_bits)))
    states = [
        pltpu.VMEM((count, block_count + PAD + (PAD if index == level_count else 0), LANES), jnp.float32)
        for index, count in enumerate(counts)
    ]
    peaks = pl.pallas_call(
        functools.partial(kernel, subbands, chunks),
        out_shape=jax.ShapeDtypeStruct((row_count, prof_count, block_count), jnp.bfloat16),
        in_specs=[
            pl.BlockSpec(memory_space=pltpu.HBM),
            pl.BlockSpec(memory_space=pltpu.HBM),
            pl.BlockSpec(memory_space=pltpu.HBM),
        ],
        out_specs=pl.BlockSpec(memory_space=pltpu.VMEM),
        scratch_shapes=[
            pltpu.VMEM(spectra.shape, spectra.dtype),
            pltpu.VMEM(profiles.shape, profiles.dtype),
            pltpu.SMEM(shifts.shape, shifts.dtype),
            pltpu.SemaphoreType.DMA((len(chunks) + 2,)),
            pltpu.VMEM((row_count * block_count, LANES), jnp.float32),
            pltpu.VMEM((HOLD * prof_count, span_len), jnp.bfloat16),
            pltpu.VMEM((1, LANES), jnp.float32),
            pltpu.VMEM((subbands, 1, LANES), jnp.float32),
            *[pltpu.VMEM((subbands, size, LANES), jnp.float32) for _, size, _, _ in chunks],
            *states,
            pltpu.SemaphoreType.DMA((len(chunks),)),
            pltpu.SemaphoreType.DMA((len(chunks),)),
            pltpu.SemaphoreType.DMA,
            pltpu.SemaphoreType.DMA,
        ],
        compiler_params=pltpu.CompilerParams(
            collective_id=0, has_side_effects=True, vmem_limit_bytes=40 * 2**20
        ),
        name="merge_and_correlate",
    )(*[pltpu.with_memory_space_constraint(array, pltpu.HBM) for array in (spectra, profiles, shifts)])
    return peaks


def solution(mesh):
    in_specs = (P(("beam", "freq"), None), P(), P())
    out_specs = P(("beam", "freq"), None, None)
    return jax.shard_map(
        per_device, mesh=mesh, in_specs=in_specs, out_specs=out_specs, check_vma=False
    )
```

```python
import functools

import jax
import jax.numpy as jnp
from jax import lax
from jax.experimental import pallas as pl
from jax.experimental.pallas import tpu as pltpu
from jax.sharding import PartitionSpec as P

STRIDE = 8
HOLD = 16
LANES = STRIDE * HOLD
PAD = 8


TAIL = 16


def chunk_plan(block_count):
    first = block_count - TAIL
    return [(0, first, 0, first - PAD), (first, TAIL, first - PAD, TAIL + PAD)]


def row_base(device_index, level, level_count, row_bits):
    base = 0
    for place in range(row_bits):
        if level + place < level_count:
            base = base + ((device_index // 2 ** (level + place)) % 2) * 2 ** (row_bits - 1 - place)
    return base


def kernel(
    subbands, chunks, spectra_hbm, profiles_hbm, shifts_hbm, out_ref,
    spectra_ref, profiles_ref, shifts_ref, load_sem, source, table, power_out, power_in, *rest,
):
    received, rest = rest[: len(chunks)], rest[len(chunks) :]
    level_count = subbands.bit_length() - 1
    states = rest[: level_count + 1]
    send_sem, recv_sem, power_send, power_recv = rest[level_count + 1 :]
    row_count, time_len = spectra_ref.shape
    row_bits = row_count.bit_length() - 1
    block_count = time_len // LANES
    prof_count, tap_count = profiles_ref.shape
    me = lax.axis_index("freq")

    my_row = row_base(me, 0, level_count, row_bits)

    flips = [1 - 2 * ((me // 2**bit) % 2) for bit in range(level_count)]

    def peer_at(distance):
        peer, row = me, my_row
        for bit in range(level_count):
            differs = (distance // 2**bit) % 2
            if isinstance(differs, int) and not differs:
                continue
            peer = peer + differs * 2**bit * flips[bit]
            if bit < row_bits:
                row = row + differs * 2 ** (row_bits - 1 - bit) * flips[bit]
        return peer, row

    def for_peers(send):
        half = subbands // 2

        def step(near, carry):
            send(half + near)
            send(near)
            return carry

        send(half)
        if subbands <= 16:
            for near in range(1, half):
                step(near, 0)
        else:
            lax.fori_loop(1, half, step, 0)

    barrier = pltpu.get_barrier_semaphore()

    def greet(distance):
        pl.semaphore_signal(
            barrier,
            inc=1,
            device_id={"freq": peer_at(distance)[0]},
            device_id_type=pl.DeviceIdType.MESH,
        )

    loads = [
        pltpu.make_async_copy(
            spectra_hbm.at[:, pl.ds(start * LANES, size * LANES)],
            spectra_ref.at[:, pl.ds(start * LANES, size * LANES)],
            load_sem.at[index],
        )
        for index, (start, size, _, _) in enumerate(chunks)
    ]
    loads.append(pltpu.make_async_copy(profiles_hbm, profiles_ref, load_sem.at[len(chunks)]))
    loads.append(pltpu.make_async_copy(shifts_hbm, shifts_ref, load_sem.at[len(chunks) + 1]))
    loads[0].start()
    for_peers(greet)
    for load in loads[1:]:
        load.start()

    for state in states:
        state[:, 0:PAD, :] = jnp.zeros((state.shape[0], PAD, LANES), jnp.float32)
    last = states[-1]
    last[:, PAD + block_count :, :] = jnp.zeros((row_count, PAD, LANES), jnp.float32)

    total_power = [jnp.zeros((row_count, LANES), jnp.float32)]

    def lay_out(index):
        start, size, _, _ = chunks[index]
        loads[index].wait()
        power = total_power[0]
        for block in range(start, start + size):
            piece = spectra_ref[:, block * LANES : (block + 1) * LANES]
            power = power + piece * piece
            source[pl.ds(block, row_count, stride=block_count), :] = piece
        total_power[0] = power

    def send_chunk(index):
        start, size, _, _ = chunks[index]
        inbox = received[index]

        def send(distance):
            peer, row = peer_at(distance)
            first = pl.multiple_of(row * block_count + start, 8)
            pltpu.make_async_remote_copy(
                src_ref=source.at[pl.ds(first, size), :],
                dst_ref=inbox.at[me],
                send_sem=send_sem.at[index],
                recv_sem=recv_sem.at[index],
                device_id={"freq": peer},
                device_id_type=pl.DeviceIdType.MESH,
            ).start()

        for_peers(send)
        mine = pl.multiple_of(my_row * block_count + start, 8)
        inbox[me] = source[pl.ds(mine, size), :]

    def send_power(distance):
        peer, _ = peer_at(distance)
        pltpu.make_async_remote_copy(
            src_ref=power_out,
            dst_ref=power_in.at[me],
            send_sem=power_send,
            recv_sem=power_recv,
            device_id={"freq": peer},
            device_id_type=pl.DeviceIdType.MESH,
        ).start()

    lay_out(0)
    pl.semaphore_wait(barrier, subbands - 1)
    send_chunk(0)
    lay_out(1)
    power_out[...] = jnp.sum(total_power[0], axis=0, keepdims=True)
    for_peers(send_power)
    power_in[me] = power_out[...]
    send_chunk(1)

    loads[len(chunks)].wait()
    span_len = table.shape[1]
    padded = jnp.concatenate(
        [profiles_ref[...].astype(jnp.float32), jnp.zeros((prof_count, span_len - tap_count), jnp.float32)],
        axis=1,
    )
    for offset in range(HOLD):
        moved = pltpu.roll(padded, offset * STRIDE, 1) if offset else padded
        table[offset * prof_count : (offset + 1) * prof_count, :] = moved.astype(jnp.bfloat16)

    lane = lax.broadcasted_iota(jnp.int32, (1, LANES), 1)
    others = subbands - 1
    lane_bits = LANES.bit_length() - 1

    def wait_for(ref, sem):
        view = ref.at[pl.ds(0, others)]
        pltpu.make_async_copy(view, view, sem).wait()

    loads[len(chunks) + 1].wait()
    scale = None
    for index, (start, size, place, part) in enumerate(chunks):
        inbox = received[index]
        wait_for(inbox, recv_sem.at[index])
        rows = pl.ds(PAD + start, size)
        for pair in range(subbands // 2):
            states[0][pair, rows, :] = inbox[2 * pair + 1]
        for level in range(level_count):
            free = max(0, level + 1 - (level_count - row_bits))
            width = 2**free
            above = 2 ** max(0, level - (level_count - row_bits))
            base = ((me // 2**level) % 2) * row_count + row_base(
                me, level + 1, level_count, row_bits
            )
            for group in range(subbands >> (level + 1)):
                node = subbands - (subbands >> level) + group
                for row in range(width):
                    parent = row // 2 if free else 0
                    delay = shifts_ref[node, base + row]
                    whole, rest_len = delay >> lane_bits, delay & (LANES - 1)
                    if level == 0:
                        low = inbox[2 * group]
                        high_index = group
                    else:
                        low = states[level][2 * group * above + parent, rows, :]
                        high_index = (2 * group + 1) * above + parent
                    near = states[level][high_index, pl.ds(PAD + start - whole, size), :]
                    far = states[level][high_index, pl.ds(PAD - 1 + start - whole, size), :]
                    mixed = jnp.where(lane < LANES - rest_len, near, far)
                    states[level + 1][group * width + row, rows, :] = low + pltpu.roll(mixed, rest_len, 1)
        first = PAD + place
        pieces = [
            last[:, first + extra : first + extra + part, :]
            .reshape(row_count * part, LANES)
            .astype(jnp.bfloat16)
            for extra in range(span_len // LANES)
        ]
        windows = jnp.concatenate(pieces, axis=1)
        tops = []
        for left in range(0, row_count * part, 2 * LANES):
            product = lax.dot_general(
                table[...],
                windows[left : left + 2 * LANES],
                (((1,), (1,)), ((), ())),
                preferred_element_type=jnp.float32,
            )
            tops.append(jnp.max(product.reshape(HOLD, prof_count, product.shape[1]), axis=0))
        best = jnp.concatenate(tops, axis=1)
        if index == 0:
            wait_for(power_in, power_recv)
            total = jnp.sum(jnp.sum(power_in[...], axis=0), axis=1, keepdims=True)
            rms_level = jnp.sqrt(
                subbands * total / (subbands * row_count * time_len) + 1e-06
            )
            scale = 1.0 / rms_level
        scaled = (best * scale).astype(jnp.bfloat16)
        for row in range(row_count):
            out_ref[row, :, place : place + part] = scaled[:, row * part : (row + 1) * part]

    for index in range(len(chunks)):
        wait_for(received[index], send_sem.at[index])
    wait_for(power_in, power_send)


def per_device(spectra, profiles, shifts):
    row_count, time_len = spectra.shape
    prof_count, tap_count = profiles.shape
    subbands = lax.axis_size("freq")
    level_count = subbands.bit_length() - 1
    row_bits = row_count.bit_length() - 1
    block_count = time_len // LANES
    chunks = chunk_plan(block_count)
    extra = (tap_count + LANES - STRIDE - 1) // LANES
    span_len = (extra + 1) * LANES
    counts = [subbands // 2]
    for level in range(1, level_count + 1):
        counts.append((subbands >> level) * 2 ** max(0, level - (level_count - row_bits)))
    states = [
        pltpu.VMEM((count, block_count + PAD + (PAD if index == level_count else 0), LANES), jnp.float32)
        for index, count in enumerate(counts)
    ]
    peaks = pl.pallas_call(
        functools.partial(kernel, subbands, chunks),
        out_shape=jax.ShapeDtypeStruct((row_count, prof_count, block_count), jnp.bfloat16),
        in_specs=[
            pl.BlockSpec(memory_space=pltpu.HBM),
            pl.BlockSpec(memory_space=pltpu.HBM),
            pl.BlockSpec(memory_space=pltpu.HBM),
        ],
        out_specs=pl.BlockSpec(memory_space=pltpu.VMEM),
        scratch_shapes=[
            pltpu.VMEM(spectra.shape, spectra.dtype),
            pltpu.VMEM(profiles.shape, profiles.dtype),
            pltpu.SMEM(shifts.shape, shifts.dtype),
            pltpu.SemaphoreType.DMA((len(chunks) + 2,)),
            pltpu.VMEM((row_count * block_count, LANES), jnp.float32),
            pltpu.VMEM((HOLD * prof_count, span_len), jnp.bfloat16),
            pltpu.VMEM((1, LANES), jnp.float32),
            pltpu.VMEM((subbands, 1, LANES), jnp.float32),
            *[pltpu.VMEM((subbands, size, LANES), jnp.float32) for _, size, _, _ in chunks],
            *states,
            pltpu.SemaphoreType.DMA((len(chunks),)),
            pltpu.SemaphoreType.DMA((len(chunks),)),
            pltpu.SemaphoreType.DMA,
            pltpu.SemaphoreType.DMA,
        ],
        compiler_params=pltpu.CompilerParams(
            collective_id=0, has_side_effects=True, vmem_limit_bytes=40 * 2**20
        ),
        name="merge_and_correlate",
    )(*[pltpu.with_memory_space_constraint(array, pltpu.HBM) for array in (spectra, profiles, shifts)])
    return peaks


def solution(mesh):
    in_specs = (P(("beam", "freq"), None), P(), P())
    out_specs = P(("beam", "freq"), None, None)
    return jax.shard_map(
        per_device, mesh=mesh, in_specs=in_specs, out_specs=out_specs, check_vma=False
    )
```

```python
import functools

import jax
import jax.numpy as jnp
from jax import lax
from jax.experimental import pallas as pl
from jax.experimental.pallas import tpu as pltpu
from jax.sharding import PartitionSpec as P

STRIDE = 8
HOLD = 16
LANES = STRIDE * HOLD
PAD = 8


TAIL = 8


def chunk_plan(block_count):
    first = block_count - TAIL
    return [(0, first, 0, first - PAD), (first, TAIL, first - PAD, TAIL + PAD)]


def row_base(device_index, level, level_count, row_bits):
    base = 0
    for place in range(row_bits):
        if level + place < level_count:
            base = base + ((device_index // 2 ** (level + place)) % 2) * 2 ** (row_bits - 1 - place)
    return base


def kernel(
    subbands, chunks, spectra_hbm, profiles_hbm, shifts_hbm, out_ref,
    spectra_ref, profiles_ref, shifts_ref, load_sem, source, table, power_out, power_in, *rest,
):
    received, rest = rest[: len(chunks)], rest[len(chunks) :]
    level_count = subbands.bit_length() - 1
    states = rest[: level_count + 1]
    send_sem, recv_sem, power_send, power_recv = rest[level_count + 1 :]
    row_count, time_len = spectra_ref.shape
    row_bits = row_count.bit_length() - 1
    block_count = time_len // LANES
    prof_count, tap_count = profiles_ref.shape
    me = lax.axis_index("freq")

    my_row = row_base(me, 0, level_count, row_bits)

    flips = [1 - 2 * ((me // 2**bit) % 2) for bit in range(level_count)]

    def peer_at(distance):
        peer, row = me, my_row
        for bit in range(level_count):
            differs = (distance // 2**bit) % 2
            if isinstance(differs, int) and not differs:
                continue
            peer = peer + differs * 2**bit * flips[bit]
            if bit < row_bits:
                row = row + differs * 2 ** (row_bits - 1 - bit) * flips[bit]
        return peer, row

    def for_peers(send):
        half = subbands // 2

        def step(near, carry):
            send(half + near)
            send(near)
            return carry

        send(half)
        if subbands <= 16:
            for near in range(1, half):
                step(near, 0)
        else:
            lax.fori_loop(1, half, step, 0)

    barrier = pltpu.get_barrier_semaphore()

    def greet(distance):
        pl.semaphore_signal(
            barrier,
            inc=1,
            device_id={"freq": peer_at(distance)[0]},
            device_id_type=pl.DeviceIdType.MESH,
        )

    loads = [
        pltpu.make_async_copy(
            spectra_hbm.at[:, pl.ds(start * LANES, size * LANES)],
            spectra_ref.at[:, pl.ds(start * LANES, size * LANES)],
            load_sem.at[index],
        )
        for index, (start, size, _, _) in enumerate(chunks)
    ]
    loads.append(pltpu.make_async_copy(profiles_hbm, profiles_ref, load_sem.at[len(chunks)]))
    loads.append(pltpu.make_async_copy(shifts_hbm, shifts_ref, load_sem.at[len(chunks) + 1]))
    loads[0].start()
    for_peers(greet)
    for load in loads[1:]:
        load.start()

    for state in states:
        state[:, 0:PAD, :] = jnp.zeros((state.shape[0], PAD, LANES), jnp.float32)
    last = states[-1]
    last[:, PAD + block_count :, :] = jnp.zeros((row_count, PAD, LANES), jnp.float32)

    total_power = [jnp.zeros((row_count, LANES), jnp.float32)]

    def lay_out(index):
        start, size, _, _ = chunks[index]
        loads[index].wait()
        power = total_power[0]
        for block in range(start, start + size):
            piece = spectra_ref[:, block * LANES : (block + 1) * LANES]
            power = power + piece * piece
            source[pl.ds(block, row_count, stride=block_count), :] = piece
        total_power[0] = power

    def send_chunk(index):
        start, size, _, _ = chunks[index]
        inbox = received[index]

        def send(distance):
            peer, row = peer_at(distance)
            first = pl.multiple_of(row * block_count + start, 8)
            pltpu.make_async_remote_copy(
                src_ref=source.at[pl.ds(first, size), :],
                dst_ref=inbox.at[me],
                send_sem=send_sem.at[index],
                recv_sem=recv_sem.at[index],
                device_id={"freq": peer},
                device_id_type=pl.DeviceIdType.MESH,
            ).start()

        for_peers(send)
        mine = pl.multiple_of(my_row * block_count + start, 8)
        inbox[me] = source[pl.ds(mine, size), :]

    def send_power(distance):
        peer, _ = peer_at(distance)
        pltpu.make_async_remote_copy(
            src_ref=power_out,
            dst_ref=power_in.at[me],
            send_sem=power_send,
            recv_sem=power_recv,
            device_id={"freq": peer},
            device_id_type=pl.DeviceIdType.MESH,
        ).start()

    lay_out(0)
    pl.semaphore_wait(barrier, subbands - 1)
    send_chunk(0)
    lay_out(1)
    power_out[...] = jnp.sum(total_power[0], axis=0, keepdims=True)
    for_peers(send_power)
    power_in[me] = power_out[...]
    send_chunk(1)

    loads[len(chunks)].wait()
    span_len = table.shape[1]
    padded = jnp.concatenate(
        [profiles_ref[...].astype(jnp.float32), jnp.zeros((prof_count, span_len - tap_count), jnp.float32)],
        axis=1,
    )
    for offset in range(HOLD):
        moved = pltpu.roll(padded, offset * STRIDE, 1) if offset else padded
        table[offset * prof_count : (offset + 1) * prof_count, :] = moved.astype(jnp.bfloat16)

    lane = lax.broadcasted_iota(jnp.int32, (1, LANES), 1)
    others = subbands - 1
    lane_bits = LANES.bit_length() - 1

    def wait_for(ref, sem):
        view = ref.at[pl.ds(0, others)]
        pltpu.make_async_copy(view, view, sem).wait()

    loads[len(chunks) + 1].wait()
    scale = None
    for index, (start, size, place, part) in enumerate(chunks):
        inbox = received[index]
        wait_for(inbox, recv_sem.at[index])
        rows = pl.ds(PAD + start, size)
        for pair in range(subbands // 2):
            states[0][pair, rows, :] = inbox[2 * pair + 1]
        for level in range(level_count):
            free = max(0, level + 1 - (level_count - row_bits))
            width = 2**free
            above = 2 ** max(0, level - (level_count - row_bits))
            base = ((me // 2**level) % 2) * row_count + row_base(
                me, level + 1, level_count, row_bits
            )
            for group in range(subbands >> (level + 1)):
                node = subbands - (subbands >> level) + group
                for row in range(width):
                    parent = row // 2 if free else 0
                    delay = shifts_ref[node, base + row]
                    whole, rest_len = delay >> lane_bits, delay & (LANES - 1)
                    if level == 0:
                        low = inbox[2 * group]
                        high_index = group
                    else:
                        low = states[level][2 * group * above + parent, rows, :]
                        high_index = (2 * group + 1) * above + parent
                    near = states[level][high_index, pl.ds(PAD + start - whole, size), :]
                    far = states[level][high_index, pl.ds(PAD - 1 + start - whole, size), :]
                    mixed = jnp.where(lane < LANES - rest_len, near, far)
                    states[level + 1][group * width + row, rows, :] = low + pltpu.roll(mixed, rest_len, 1)
        first = PAD + place
        pieces = [
            last[:, first + extra : first + extra + part, :]
            .reshape(row_count * part, LANES)
            .astype(jnp.bfloat16)
            for extra in range(span_len // LANES)
        ]
        windows = jnp.concatenate(pieces, axis=1)
        tops = []
        for left in range(0, row_count * part, 2 * LANES):
            product = lax.dot_general(
                table[...],
                windows[left : left + 2 * LANES],
                (((1,), (1,)), ((), ())),
                preferred_element_type=jnp.float32,
            )
            tops.append(jnp.max(product.reshape(HOLD, prof_count, product.shape[1]), axis=0))
        best = jnp.concatenate(tops, axis=1)
        if index == 0:
            wait_for(power_in, power_recv)
            total = jnp.sum(jnp.sum(power_in[...], axis=0), axis=1, keepdims=True)
            rms_level = jnp.sqrt(
                subbands * total / (subbands * row_count * time_len) + 1e-06
            )
            scale = 1.0 / rms_level
        scaled = (best * scale).astype(jnp.bfloat16)
        for row in range(row_count):
            out_ref[row, :, place : place + part] = scaled[:, row * part : (row + 1) * part]

    for index in range(len(chunks)):
        wait_for(received[index], send_sem.at[index])
    wait_for(power_in, power_send)


def per_device(spectra, profiles, shifts):
    row_count, time_len = spectra.shape
    prof_count, tap_count = profiles.shape
    subbands = lax.axis_size("freq")
    level_count = subbands.bit_length() - 1
    row_bits = row_count.bit_length() - 1
    block_count = time_len // LANES
    chunks = chunk_plan(block_count)
    extra = (tap_count + LANES - STRIDE - 1) // LANES
    span_len = (extra + 1) * LANES
    counts = [subbands // 2]
    for level in range(1, level_count + 1):
        counts.append((subbands >> level) * 2 ** max(0, level - (level_count - row_bits)))
    states = [
        pltpu.VMEM((count, block_count + PAD + (PAD if index == level_count else 0), LANES), jnp.float32)
        for index, count in enumerate(counts)
    ]
    peaks = pl.pallas_call(
        functools.partial(kernel, subbands, chunks),
        out_shape=jax.ShapeDtypeStruct((row_count, prof_count, block_count), jnp.bfloat16),
        in_specs=[
            pl.BlockSpec(memory_space=pltpu.HBM),
            pl.BlockSpec(memory_space=pltpu.HBM),
            pl.BlockSpec(memory_space=pltpu.HBM),
        ],
        out_specs=pl.BlockSpec(memory_space=pltpu.VMEM),
        scratch_shapes=[
            pltpu.VMEM(spectra.shape, spectra.dtype),
            pltpu.VMEM(profiles.shape, profiles.dtype),
            pltpu.SMEM(shifts.shape, shifts.dtype),
            pltpu.SemaphoreType.DMA((len(chunks) + 2,)),
            pltpu.VMEM((row_count * block_count, LANES), jnp.float32),
            pltpu.VMEM((HOLD * prof_count, span_len), jnp.bfloat16),
            pltpu.VMEM((1, LANES), jnp.float32),
            pltpu.VMEM((subbands, 1, LANES), jnp.float32),
            *[pltpu.VMEM((subbands, size, LANES), jnp.float32) for _, size, _, _ in chunks],
            *states,
            pltpu.SemaphoreType.DMA((len(chunks),)),
            pltpu.SemaphoreType.DMA((len(chunks),)),
            pltpu.SemaphoreType.DMA,
            pltpu.SemaphoreType.DMA,
        ],
        compiler_params=pltpu.CompilerParams(
            collective_id=0, has_side_effects=True, vmem_limit_bytes=40 * 2**20
        ),
        name="merge_and_correlate",
    )(*[pltpu.with_memory_space_constraint(array, pltpu.HBM) for array in (spectra, profiles, shifts)])
    return peaks


def solution(mesh):
    in_specs = (P(("beam", "freq"), None), P(), P())
    out_specs = P(("beam", "freq"), None, None)
    return jax.shard_map(
        per_device, mesh=mesh, in_specs=in_specs, out_specs=out_specs, check_vma=False
    )
```

```python
import functools

import jax
import jax.numpy as jnp
from jax import lax
from jax.experimental import pallas as pl
from jax.experimental.pallas import tpu as pltpu
from jax.sharding import PartitionSpec as P

STRIDE = 8
HOLD = 16
LANES = STRIDE * HOLD
PAD = 8


TAIL = 24


def chunk_plan(block_count):
    first = block_count - TAIL
    return [(0, first, 0, first - PAD), (first, TAIL, first - PAD, TAIL + PAD)]


def row_base(device_index, level, level_count, row_bits):
    base = 0
    for place in range(row_bits):
        if level + place < level_count:
            base = base + ((device_index // 2 ** (level + place)) % 2) * 2 ** (row_bits - 1 - place)
    return base


def kernel(
    subbands, chunks, spectra_hbm, profiles_hbm, shifts_hbm, out_ref,
    spectra_ref, profiles_ref, shifts_ref, load_sem, source, table, power_out, power_in, *rest,
):
    received, rest = rest[: len(chunks)], rest[len(chunks) :]
    level_count = subbands.bit_length() - 1
    states = rest[: level_count + 1]
    send_sem, recv_sem, power_send, power_recv = rest[level_count + 1 :]
    row_count, time_len = spectra_ref.shape
    row_bits = row_count.bit_length() - 1
    block_count = time_len // LANES
    prof_count, tap_count = profiles_ref.shape
    me = lax.axis_index("freq")

    my_row = row_base(me, 0, level_count, row_bits)

    flips = [1 - 2 * ((me // 2**bit) % 2) for bit in range(level_count)]

    def peer_at(distance):
        peer, row = me, my_row
        for bit in range(level_count):
            differs = (distance // 2**bit) % 2
            if isinstance(differs, int) and not differs:
                continue
            peer = peer + differs * 2**bit * flips[bit]
            if bit < row_bits:
                row = row + differs * 2 ** (row_bits - 1 - bit) * flips[bit]
        return peer, row

    def for_peers(send):
        half = subbands // 2

        def step(near, carry):
            send(half + near)
            send(near)
            return carry

        send(half)
        if subbands <= 16:
            for near in range(1, half):
                step(near, 0)
        else:
            lax.fori_loop(1, half, step, 0)

    barrier = pltpu.get_barrier_semaphore()

    def greet(distance):
        pl.semaphore_signal(
            barrier,
            inc=1,
            device_id={"freq": peer_at(distance)[0]},
            device_id_type=pl.DeviceIdType.MESH,
        )

    loads = [
        pltpu.make_async_copy(
            spectra_hbm.at[:, pl.ds(start * LANES, size * LANES)],
            spectra_ref.at[:, pl.ds(start * LANES, size * LANES)],
            load_sem.at[index],
        )
        for index, (start, size, _, _) in enumerate(chunks)
    ]
    loads.append(pltpu.make_async_copy(profiles_hbm, profiles_ref, load_sem.at[len(chunks)]))
    loads.append(pltpu.make_async_copy(shifts_hbm, shifts_ref, load_sem.at[len(chunks) + 1]))
    loads[0].start()
    for_peers(greet)
    for load in loads[1:]:
        load.start()

    for state in states:
        state[:, 0:PAD, :] = jnp.zeros((state.shape[0], PAD, LANES), jnp.float32)
    last = states[-1]
    last[:, PAD + block_count :, :] = jnp.zeros((row_count, PAD, LANES), jnp.float32)

    total_power = [jnp.zeros((row_count, LANES), jnp.float32)]

    def lay_out(index):
        start, size, _, _ = chunks[index]
        loads[index].wait()
        power = total_power[0]
        for block in range(start, start + size):
            piece = spectra_ref[:, block * LANES : (block + 1) * LANES]
            power = power + piece * piece
            source[pl.ds(block, row_count, stride=block_count), :] = piece
        total_power[0] = power

    def send_chunk(index):
        start, size, _, _ = chunks[index]
        inbox = received[index]

        def send(distance):
            peer, row = peer_at(distance)
            first = pl.multiple_of(row * block_count + start, 8)
            pltpu.make_async_remote_copy(
                src_ref=source.at[pl.ds(first, size), :],
                dst_ref=inbox.at[me],
                send_sem=send_sem.at[index],
                recv_sem=recv_sem.at[index],
                device_id={"freq": peer},
                device_id_type=pl.DeviceIdType.MESH,
            ).start()

        for_peers(send)
        mine = pl.multiple_of(my_row * block_count + start, 8)
        inbox[me] = source[pl.ds(mine, size), :]

    def send_power(distance):
        peer, _ = peer_at(distance)
        pltpu.make_async_remote_copy(
            src_ref=power_out,
            dst_ref=power_in.at[me],
            send_sem=power_send,
            recv_sem=power_recv,
            device_id={"freq": peer},
            device_id_type=pl.DeviceIdType.MESH,
        ).start()

    lay_out(0)
    pl.semaphore_wait(barrier, subbands - 1)
    send_chunk(0)
    lay_out(1)
    power_out[...] = jnp.sum(total_power[0], axis=0, keepdims=True)
    for_peers(send_power)
    power_in[me] = power_out[...]
    send_chunk(1)

    loads[len(chunks)].wait()
    span_len = table.shape[1]
    padded = jnp.concatenate(
        [profiles_ref[...].astype(jnp.float32), jnp.zeros((prof_count, span_len - tap_count), jnp.float32)],
        axis=1,
    )
    for offset in range(HOLD):
        moved = pltpu.roll(padded, offset * STRIDE, 1) if offset else padded
        table[offset * prof_count : (offset + 1) * prof_count, :] = moved.astype(jnp.bfloat16)

    lane = lax.broadcasted_iota(jnp.int32, (1, LANES), 1)
    others = subbands - 1
    lane_bits = LANES.bit_length() - 1

    def wait_for(ref, sem):
        view = ref.at[pl.ds(0, others)]
        pltpu.make_async_copy(view, view, sem).wait()

    loads[len(chunks) + 1].wait()
    scale = None
    for index, (start, size, place, part) in enumerate(chunks):
        inbox = received[index]
        wait_for(inbox, recv_sem.at[index])
        rows = pl.ds(PAD + start, size)
        for pair in range(subbands // 2):
            states[0][pair, rows, :] = inbox[2 * pair + 1]
        for level in range(level_count):
            free = max(0, level + 1 - (level_count - row_bits))
            width = 2**free
            above = 2 ** max(0, level - (level_count - row_bits))
            base = ((me // 2**level) % 2) * row_count + row_base(
                me, level + 1, level_count, row_bits
            )
            for group in range(subbands >> (level + 1)):
                node = subbands - (subbands >> level) + group
                for row in range(width):
                    parent = row // 2 if free else 0
                    delay = shifts_ref[node, base + row]
                    whole, rest_len = delay >> lane_bits, delay & (LANES - 1)
                    if level == 0:
                        low = inbox[2 * group]
                        high_index = group
                    else:
                        low = states[level][2 * group * above + parent, rows, :]
                        high_index = (2 * group + 1) * above + parent
                    near = states[level][high_index, pl.ds(PAD + start - whole, size), :]
                    far = states[level][high_index, pl.ds(PAD - 1 + start - whole, size), :]
                    mixed = jnp.where(lane < LANES - rest_len, near, far)
                    states[level + 1][group * width + row, rows, :] = low + pltpu.roll(mixed, rest_len, 1)
        first = PAD + place
        pieces = [
            last[:, first + extra : first + extra + part, :]
            .reshape(row_count * part, LANES)
            .astype(jnp.bfloat16)
            for extra in range(span_len // LANES)
        ]
        windows = jnp.concatenate(pieces, axis=1)
        tops = []
        for left in range(0, row_count * part, 2 * LANES):
            product = lax.dot_general(
                table[...],
                windows[left : left + 2 * LANES],
                (((1,), (1,)), ((), ())),
                preferred_element_type=jnp.float32,
            )
            tops.append(jnp.max(product.reshape(HOLD, prof_count, product.shape[1]), axis=0))
        best = jnp.concatenate(tops, axis=1)
        if index == 0:
            wait_for(power_in, power_recv)
            total = jnp.sum(jnp.sum(power_in[...], axis=0), axis=1, keepdims=True)
            rms_level = jnp.sqrt(
                subbands * total / (subbands * row_count * time_len) + 1e-06
            )
            scale = 1.0 / rms_level
        scaled = (best * scale).astype(jnp.bfloat16)
        for row in range(row_count):
            out_ref[row, :, place : place + part] = scaled[:, row * part : (row + 1) * part]

    for index in range(len(chunks)):
        wait_for(received[index], send_sem.at[index])
    wait_for(power_in, power_send)


def per_device(spectra, profiles, shifts):
    row_count, time_len = spectra.shape
    prof_count, tap_count = profiles.shape
    subbands = lax.axis_size("freq")
    level_count = subbands.bit_length() - 1
    row_bits = row_count.bit_length() - 1
    block_count = time_len // LANES
    chunks = chunk_plan(block_count)
    extra = (tap_count + LANES - STRIDE - 1) // LANES
    span_len = (extra + 1) * LANES
    counts = [subbands // 2]
    for level in range(1, level_count + 1):
        counts.append((subbands >> level) * 2 ** max(0, level - (level_count - row_bits)))
    states = [
        pltpu.VMEM((count, block_count + PAD + (PAD if index == level_count else 0), LANES), jnp.float32)
        for index, count in enumerate(counts)
    ]
    peaks = pl.pallas_call(
        functools.partial(kernel, subbands, chunks),
        out_shape=jax.ShapeDtypeStruct((row_count, prof_count, block_count), jnp.bfloat16),
        in_specs=[
            pl.BlockSpec(memory_space=pltpu.HBM),
            pl.BlockSpec(memory_space=pltpu.HBM),
            pl.BlockSpec(memory_space=pltpu.HBM),
        ],
        out_specs=pl.BlockSpec(memory_space=pltpu.VMEM),
        scratch_shapes=[
            pltpu.VMEM(spectra.shape, spectra.dtype),
            pltpu.VMEM(profiles.shape, profiles.dtype),
            pltpu.SMEM(shifts.shape, shifts.dtype),
            pltpu.SemaphoreType.DMA((len(chunks) + 2,)),
            pltpu.VMEM((row_count * block_count, LANES), jnp.float32),
            pltpu.VMEM((HOLD * prof_count, span_len), jnp.bfloat16),
            pltpu.VMEM((1, LANES), jnp.float32),
            pltpu.VMEM((subbands, 1, LANES), jnp.float32),
            *[pltpu.VMEM((subbands, size, LANES), jnp.float32) for _, size, _, _ in chunks],
            *states,
            pltpu.SemaphoreType.DMA((len(chunks),)),
            pltpu.SemaphoreType.DMA((len(chunks),)),
            pltpu.SemaphoreType.DMA,
            pltpu.SemaphoreType.DMA,
        ],
        compiler_params=pltpu.CompilerParams(
            collective_id=0, has_side_effects=True, vmem_limit_bytes=40 * 2**20
        ),
        name="merge_and_correlate",
    )(*[pltpu.with_memory_space_constraint(array, pltpu.HBM) for array in (spectra, profiles, shifts)])
    return peaks


def solution(mesh):
    in_specs = (P(("beam", "freq"), None), P(), P())
    out_specs = P(("beam", "freq"), None, None)
    return jax.shard_map(
        per_device, mesh=mesh, in_specs=in_specs, out_specs=out_specs, check_vma=False
    )
```
